32 devices in a mesh: dp: 8 (over z, y), shard: 4 (over x, core).
Axes of the slice: x: 2, y: 2, z: 4, core: 2. Of those that a mesh axis runs over, the one named last changes fastest.
Arguments:
- tokens: bfloat16 [4, 1024, 960], P('shard', 'dp'), may hold values from -6 to 6
- cotangent: bfloat16 [4, 1024, 960], P('shard', 'dp'), may hold values from -6 to 6
- seq_lengths: int32 [4, 2], P('shard'), may hold values from 1 to 512, as said below
- block_slot: int32 [4, 8], P('shard'), may hold values from 0 to 7, as said below
- qkv_master: float32 [960, 1600], P('shard', 'dp'), may hold values from -0.1875 to 0.1875
- qkv_first: float32 [960, 1600], P('shard', 'dp'), may hold values from -6 to 6
- qkv_second: float32 [960, 1600], P('shard', 'dp'), may hold values from 3.19488 to 51.6096
- out_master: float32 [960, 960], P('shard', 'dp'), may hold values from -0.75 to 0.75
- out_first: float32 [960, 960], P('shard', 'dp'), may hold values from -6 to 6
- out_second: float32 [960, 960], P('shard', 'dp'), may hold values from 3.19488 to 51.6096
- gate_up_master: float32 [960, 5120], P('shard', 'dp'), may hold values from -0.1875 to 0.1875
- gate_up_first: float32 [960, 5120], P('shard', 'dp'), may hold values from -6 to 6
- gate_up_second: float32 [960, 5120], P('shard', 'dp'), may hold values from 7.18848 to 116.1216
- down_master: float32 [2560, 960], P('shard', 'dp'), may hold values from -0.125 to 0.125
- down_first: float32 [2560, 960], P('shard', 'dp'), may hold values from -6 to 6
- down_second: float32 [2560, 960], P('shard', 'dp'), may hold values from 7.18848 to 116.1216
- gains_master: float32 [2, 960], replicated, may hold values from 0.5 to 1.5
- gains_first: float32 [2, 960], replicated, may hold values from -24 to 24
- gains_second: float32 [2, 960], replicated, may hold values from 39.0144 to 632.832
Outputs:
- layer_out: bfloat16 [4, 1024, 960], P('shard', 'dp')
- input_grad: bfloat16 [4, 1024, 960], P('shard', 'dp')
- qkv_grad: float32 [960, 1600], P('shard', 'dp')
- qkv_first_new: float32 [960, 1600], P('shard', 'dp')
- qkv_second_new: float32 [960, 1600], P('shard', 'dp')
- qkv_new: float32 [960, 1600], P('shard', 'dp')
- out_grad: float32 [960, 960], P('shard', 'dp')
- out_first_new: float32 [960, 960], P('shard', 'dp')
- out_second_new: float32 [960, 960], P('shard', 'dp')
- out_new: float32 [960, 960], P('shard', 'dp')
- gate_up_grad: float32 [960, 5120], P('shard', 'dp')
- gate_up_first_new: float32 [960, 5120], P('shard', 'dp')
- gate_up_second_new: float32 [960, 5120], P('shard', 'dp')
- gate_up_new: float32 [960, 5120], P('shard', 'dp')
- down_grad: float32 [2560, 960], P('shard', 'dp')
- down_first_new: float32 [2560, 960], P('shard', 'dp')
- down_second_new: float32 [2560, 960], P('shard', 'dp')
- down_new: float32 [2560, 960], P('shard', 'dp')
- gains_grad: float32 [2, 960], replicated
- gains_first_new: float32 [2, 960], replicated
- gains_second_new: float32 [2, 960], replicated
- gains_new: float32 [2, 960], replicated
The draws below stay inside these ranges and needn't reach their ends.
Inputs may be any that keep to these rules, and one draw needn't show every extreme that they name: `seq_lengths`: row s holds the lengths of the 2 sequences of group s; they sum to 768 and the largest is exactly 512. Each row is a permutation: logical block b of group s is stored in slot block_slot[s, b].
All inputs are finite; a program needn't handle non-finite values.
Results may differ from the reference program's by a relative error of at most 0.013.
Values may be sent and summed in bfloat16 or wider, within the bound.
A program may use at most 192 MiB of HBM per device.

```python
import math
import jax
import jax.numpy as jnp
from jax import lax

D = 960
HEADS = 15
KV_HEADS = 5
HEAD = 64
FF = 2560
BLOCK = 128
STEP = 10
NBLK = 8
NSEQ = 2
KW = 4
LMAX = 512
TOTAL = 768
N_SHARD = 4


def group_layout(key):
    counter = jnp.arange(NSEQ, dtype=jnp.int32)
    slot_index = jnp.arange(NBLK, dtype=jnp.int32)

    def one_group(group_key):
        first_key, second_key, third_key = jax.random.split(group_key, 3)
        longest = jax.random.randint(first_key, (), 0, NSEQ, dtype=jnp.int32)
        weights = jax.random.randint(second_key, (NSEQ,), 4, 9, dtype=jnp.int32)
        weights = jnp.where(counter == longest, 0, weights)
        spare_rows = TOTAL - LMAX
        shares = spare_rows * weights // jnp.sum(weights)
        shares = shares + jnp.where(counter == (longest + 1) % NSEQ, spare_rows - jnp.sum(shares), 0)
        lengths = jnp.where(counter == longest, LMAX, shares).astype(jnp.int32)
        counts = (lengths + BLOCK - 1) // BLOCK
        first_block = jnp.sum(jnp.where(counter < longest, counts, 0)).astype(jnp.int32)
        placing = jax.random.permutation(third_key, NBLK).astype(jnp.int32)
        for logical, target in ((first_block, 0), (first_block + KW // 2, NBLK // 2), (first_block + KW - 1, NBLK - 1)):
            holder = jnp.sum(jnp.where(placing == target, slot_index, 0))
            current = jnp.sum(jnp.where(slot_index == logical, placing, 0))
            placing = jnp.where(slot_index == holder, current, placing)
            placing = jnp.where(slot_index == logical, target, placing)
        return (lengths, placing.astype(jnp.int32))
    return jax.vmap(one_group)(jax.random.split(key, N_SHARD))


def draw_seq_lengths(key, part):
    lengths, placing = group_layout(key)
    return lengths


def draw_block_slot(key, part):
    lengths, placing = group_layout(key)
    return placing


def block_scale(key, shape, cuts, smallest, largest):
    def one(axis_at, shards_of):
        draws = jax.random.uniform(jax.random.fold_in(jax.random.fold_in(key, 6), axis_at), (shards_of,), jnp.float32, smallest / len(cuts), largest / len(cuts))
        return jnp.repeat(jnp.exp(draws), shape[axis_at] // shards_of).reshape((-1,) + (1,) * (len(shape) - axis_at - 1))

    level = one(*cuts[0])
    for cut in cuts[1:]:
        level = level * one(*cut)
    return level


def gaussian(own_key, dims, spread, bound, cuts=(), held_as=jnp.bfloat16):
    values = jax.random.normal(own_key, dims, jnp.float32) * spread
    if len(cuts) > 0:
        values = block_scale(own_key, dims, cuts, -0.22, 0.18) * values
    return jnp.clip(values, min=-bound, max=bound).astype(held_as)


def setup_inputs(seed: int = 0) -> dict:
    arg_keys = jax.random.split(jax.random.key(seed), 20)
    tokens = gaussian(arg_keys[0], (N_SHARD, NBLK * BLOCK, D), 1.0, 6.0, ((0, 4), (1, 8)))
    cotangent = gaussian(arg_keys[1], (N_SHARD, NBLK * BLOCK, D), 1.0, 6.0, ((0, 4), (1, 8)))
    seq_lengths = draw_seq_lengths(jax.random.fold_in(arg_keys[19], 71), 0)
    block_slot = draw_block_slot(jax.random.fold_in(arg_keys[19], 71), 0)
    qkv_master = gaussian(arg_keys[4], (D, (HEADS + 2 * KV_HEADS) * HEAD), D ** -0.5, 0.1875, ((0, 4), (1, 8)), jnp.float32)
    qkv_first = gaussian(arg_keys[5], (D, (HEADS + 2 * KV_HEADS) * HEAD), (0.0222 * (N_SHARD * TOTAL) ** 0.5), 6.0, ((0, 4), (1, 8)), jnp.float32)
    qkv_second = jnp.clip(jnp.exp(math.log(51.6096) - 2.7821582 * jax.random.uniform(arg_keys[6], (D, (HEADS + 2 * KV_HEADS) * HEAD), jnp.float32) ** block_scale(arg_keys[6], (D, (HEADS + 2 * KV_HEADS) * HEAD), ((0, 4), (1, 8)), -0.2, 0.2)), 3.19488, 51.6096)
    out_master = gaussian(arg_keys[7], (HEADS * HEAD, D), (D // 16) ** -0.5, 0.75, ((0, 4), (1, 8)), jnp.float32)
    out_first = gaussian(arg_keys[8], (HEADS * HEAD, D), (0.0222 * (N_SHARD * TOTAL) ** 0.5), 6.0, ((0, 4), (1, 8)), jnp.float32)
    out_second = jnp.clip(jnp.exp(math.log(51.6096) - 2.7821582 * jax.random.uniform(arg_keys[9], (HEADS * HEAD, D), jnp.float32) ** block_scale(arg_keys[9], (HEADS * HEAD, D), ((0, 4), (1, 8)), -0.2, 0.2)), 3.19488, 51.6096)
    gate_up_master = gaussian(arg_keys[10], (D, 2 * FF), D ** -0.5, 0.1875, ((0, 4), (1, 8)), jnp.float32)
    gate_up_first = gaussian(arg_keys[11], (D, 2 * FF), (0.0333 * (N_SHARD * TOTAL) ** 0.5), 6.0, ((0, 4), (1, 8)), jnp.float32)
    gate_up_second = jnp.clip(jnp.exp(math.log(116.1216) - 2.7821582 * jax.random.uniform(arg_keys[12], (D, 2 * FF), jnp.float32) ** block_scale(arg_keys[12], (D, 2 * FF), ((0, 4), (1, 8)), -0.2, 0.2)), 7.18848, 116.1216)
    down_master = gaussian(arg_keys[13], (FF, D), FF ** -0.5, 0.125, ((0, 4), (1, 8)), jnp.float32)
    down_first = gaussian(arg_keys[14], (FF, D), (0.0333 * (N_SHARD * TOTAL) ** 0.5), 6.0, ((0, 4), (1, 8)), jnp.float32)
    down_second = jnp.clip(jnp.exp(math.log(116.1216) - 2.7821582 * jax.random.uniform(arg_keys[15], (FF, D), jnp.float32) ** block_scale(arg_keys[15], (FF, D), ((0, 4), (1, 8)), -0.2, 0.2)), 7.18848, 116.1216)
    gains_master = jnp.clip(1.0 + 0.1 * jax.random.normal(arg_keys[16], (2, D), jnp.float32), 0.5, 1.5)
    gains_first = gaussian(arg_keys[17], (2, D), (0.0777 * (N_SHARD * TOTAL) ** 0.5), 24.0, (), jnp.float32)
    gains_second = jnp.clip(jnp.exp(jax.random.uniform(arg_keys[18], (2, D), jnp.float32, math.log(39.0144), math.log(632.832))), 39.0144, 632.832)
    return dict(tokens=tokens, cotangent=cotangent, seq_lengths=seq_lengths, block_slot=block_slot, qkv_master=qkv_master, qkv_first=qkv_first, qkv_second=qkv_second, out_master=out_master, out_first=out_first, out_second=out_second, gate_up_master=gate_up_master, gate_up_first=gate_up_first, gate_up_second=gate_up_second, down_master=down_master, down_first=down_first, down_second=down_second, gains_master=gains_master, gains_first=gains_first, gains_second=gains_second)


@jax.custom_vjp
def low(v):
    return lax.optimization_barrier(v.astype(jnp.bfloat16)).astype(jnp.float32)

@jax.custom_vjp
def low_back(v):
    return v

def low_keep(v):
    return (low(v), None)

def low_pass(kept, grad):
    return (grad,)

def back_keep(v):
    return (v, None)

def back_low(kept, grad):
    return (low(grad),)
low.defvjp(low_keep, low_pass)
low_back.defvjp(back_keep, back_low)
HIGHEST = lax.Precision.HIGHEST
NORM_EPS = 1e-05
MATRIX_RATE = 0.06
GAIN_RATE = 0.4
WEIGHT_DECAY = 0.1

def layout(lengths):
    counts = (lengths + BLOCK - 1) // BLOCK
    block_ends = jnp.cumsum(counts).astype(jnp.int32)
    block_starts = block_ends - counts
    row_index = jnp.arange(NBLK * BLOCK, dtype=jnp.int32)
    member = lax.optimization_barrier(jnp.sum((block_ends[None, :] <= (row_index // BLOCK)[:, None]).astype(jnp.int32), axis=1))
    choose = (member[:, None] == jnp.arange(NSEQ, dtype=jnp.int32)[None, :]).astype(jnp.int32)
    offset = row_index - BLOCK * lax.optimization_barrier(jnp.sum(choose * block_starts[None, :], axis=1))
    length_row = lax.optimization_barrier(jnp.sum(choose * lengths[None, :], axis=1))
    usable = (member < NSEQ) & (offset < length_row)
    labels = jnp.where(usable, member, NSEQ + row_index).astype(jnp.int32)
    position = jnp.where(usable, offset, 0).astype(jnp.int32)
    return (labels, position, usable)

def rope_tables(position):
    frequency = jnp.exp(jnp.arange(HEAD // 2, dtype=jnp.float32) * (-2.0 * math.log(10000.0) / HEAD))
    angle_grid = position.astype(jnp.float32)[:, None] * frequency[None, :]
    return (jnp.cos(angle_grid)[:, None, :], jnp.sin(angle_grid)[:, None, :])

def rotate(vectors, cosine_table, sine_table):
    middle = HEAD // 2
    lower_half = vectors[..., :middle]
    upper_half = vectors[..., middle:]
    return jnp.concatenate([lower_half * cosine_table - upper_half * sine_table, upper_half * cosine_table + lower_half * sine_table], axis=-1)

def attend(queries, keys_all, values_all, labels):
    rows_total = queries.shape[0]
    margin = (KW - 1) * BLOCK
    keys_padded = jnp.pad(keys_all, ((margin, 0), (0, 0), (0, 0)))
    values_padded = jnp.pad(values_all, ((margin, 0), (0, 0), (0, 0)))
    order = jnp.arange(rows_total, dtype=jnp.int32)
    filler = jnp.full((margin,), -1, jnp.int32)
    labels_padded = jnp.concatenate([filler, labels])
    order_padded = jnp.concatenate([filler, order])
    grouped = HEADS // KV_HEADS

    def one_block(block_index):
        start = block_index * BLOCK
        query_block = lax.dynamic_slice_in_dim(queries, start, BLOCK, 0).reshape(BLOCK, KV_HEADS, grouped, HEAD)
        key_block = lax.dynamic_slice_in_dim(keys_padded, start, KW * BLOCK, 0)
        value_block = lax.dynamic_slice_in_dim(values_padded, start, KW * BLOCK, 0)
        same_label = lax.dynamic_slice_in_dim(labels, start, BLOCK, 0)[:, None] == lax.dynamic_slice_in_dim(labels_padded, start, KW * BLOCK, 0)[None, :]
        causal = lax.dynamic_slice_in_dim(order_padded, start, KW * BLOCK, 0)[None, :] <= lax.dynamic_slice_in_dim(order, start, BLOCK, 0)[:, None]
        allowed = same_label & causal
        scores = low_back(jnp.einsum('qgrd,kgd->grqk', query_block, key_block, precision=HIGHEST)) * 0.125
        scores = jnp.where(allowed[None, None], scores, -1e+30)
        shifted = jnp.exp(scores - lax.optimization_barrier(jnp.max(scores, axis=-1, keepdims=True)))
        weights = low(shifted / lax.optimization_barrier(jnp.sum(shifted, axis=-1, keepdims=True)))
        mixed = jnp.einsum('grqk,kgd->qgrd', weights, value_block, precision=HIGHEST)
        return mixed.reshape(BLOCK, HEADS * HEAD)
    blocks_out = lax.map(jax.checkpoint(one_block), jnp.arange(rows_total // BLOCK, dtype=jnp.int32))
    return blocks_out.reshape(rows_total, HEADS * HEAD)

def layer(params, inputs, labels, position, usable):
    qkv_weight = low(params[0])
    out_weight = low(params[1])
    gate_up_weight = low(params[2])
    down_weight = low(params[3])
    gains = params[4]
    rows_total = inputs.shape[0]
    width_q = HEADS * HEAD
    width_kv = KV_HEADS * HEAD
    scale_first = lax.rsqrt(lax.optimization_barrier(jnp.mean(inputs * inputs, axis=-1, keepdims=True)) + NORM_EPS)
    normed_first = low(inputs * scale_first * gains[0])
    projected = low_back(jnp.dot(normed_first, qkv_weight, precision=HIGHEST))
    cosine_table, sine_table = rope_tables(position)
    queries = low(rotate(projected[:, :width_q].reshape(rows_total, HEADS, HEAD), cosine_table, sine_table))
    keys_all = low(rotate(projected[:, width_q:width_q + width_kv].reshape(rows_total, KV_HEADS, HEAD), cosine_table, sine_table))
    values_all = low(projected[:, width_q + width_kv:].reshape(rows_total, KV_HEADS, HEAD))
    attended = low(low_back(attend(queries, keys_all, values_all, labels)))
    hidden_state = inputs + low_back(jnp.dot(attended, out_weight, precision=HIGHEST))
    scale_second = lax.rsqrt(lax.optimization_barrier(jnp.mean(hidden_state * hidden_state, axis=-1, keepdims=True)) + NORM_EPS)
    normed_second = low(hidden_state * scale_second * gains[1])
    gate_up = low_back(jnp.dot(normed_second, gate_up_weight, precision=HIGHEST))
    activated = low(jax.nn.silu(gate_up[:, :FF]) * gate_up[:, FF:])
    return (hidden_state + jnp.dot(activated, down_weight, precision=HIGHEST)) * usable[:, None]

def adamw(master, grad, first, second, rate, decay):
    first_new = 0.9 * first + 0.1 * grad
    second_new = 0.95 * second + 0.05 * grad * grad
    update = first_new / (1.0 - 0.9 ** STEP) / (jnp.sqrt(second_new / (1.0 - 0.95 ** STEP)) + 1e-08)
    return (grad, first_new, second_new, master - rate * (update + decay * master))

def reference(tokens, cotangent, seq_lengths, block_slot, qkv_master, qkv_first, qkv_second, out_master, out_first, out_second, gate_up_master, gate_up_first, gate_up_second, down_master, down_first, down_second, gains_master, gains_first, gains_second):
    params = (qkv_master, out_master, gate_up_master, down_master, gains_master)

    def per_group(totals, group):
        token_slots, back_slots, lengths, placing = group
        labels, position, usable = layout(lengths)
        inputs = token_slots.reshape(NBLK, BLOCK, D)[placing].reshape(NBLK * BLOCK, D).astype(jnp.float32)
        upstream = back_slots.reshape(NBLK, BLOCK, D)[placing].reshape(NBLK * BLOCK, D).astype(jnp.float32)
        mask = usable.astype(jnp.float32)
        outputs, pull = jax.vjp(lambda weights, source: layer(weights, source, labels, position, mask), params, inputs)
        grads, input_back = pull(upstream)
        inverse = jnp.zeros((NBLK,), jnp.int32).at[placing].set(jnp.arange(NBLK, dtype=jnp.int32))
        out_slots = outputs.reshape(NBLK, BLOCK, D)[inverse].reshape(NBLK * BLOCK, D).astype(jnp.bfloat16)
        back_out = input_back.reshape(NBLK, BLOCK, D)[inverse].reshape(NBLK * BLOCK, D).astype(jnp.bfloat16)
        totals = jax.tree.map(lambda left, right: left + right, totals, grads)
        return (totals, (out_slots, back_out))
    zeros = jax.tree.map(jnp.zeros_like, params)
    grads, (layer_out, input_grad) = lax.scan(per_group, zeros, (tokens, cotangent, seq_lengths, block_slot))
    qkv_all = adamw(qkv_master, grads[0], qkv_first, qkv_second, MATRIX_RATE, WEIGHT_DECAY)
    out_all = adamw(out_master, grads[1], out_first, out_second, MATRIX_RATE, WEIGHT_DECAY)
    gate_up_all = adamw(gate_up_master, grads[2], gate_up_first, gate_up_second, MATRIX_RATE, WEIGHT_DECAY)
    down_all = adamw(down_master, grads[3], down_first, down_second, MATRIX_RATE, WEIGHT_DECAY)
    gains_all = adamw(gains_master, grads[4], gains_first, gains_second, GAIN_RATE, 0.0)
    return (layer_out, input_grad, qkv_all[0], qkv_all[1], qkv_all[2], qkv_all[3], out_all[0], out_all[1], out_all[2], out_all[3], gate_up_all[0], gate_up_all[1], gate_up_all[2], gate_up_all[3], down_all[0], down_all[1], down_all[2], down_all[3], gains_all[0], gains_all[1], gains_all[2], gains_all[3])
```

```python
import functools
import math

import jax
import jax.numpy as jnp
from jax import lax
from jax.experimental import pallas as pl
from jax.experimental.pallas import tpu as pltpu
from jax.sharding import PartitionSpec as P

HEADS = 15
KV_HEADS = 5
HEAD = 64
FF = 2560
BLOCK = 128
KBLK = 16
STEP = 10


NORM_EPS = 1e-05
MATRIX_RATE = 0.06
GAIN_RATE = 0.4
WEIGHT_DECAY = 0.1


def layout(lengths, blocks_total):
    seq_count = lengths.shape[0]
    counts = (lengths + BLOCK - 1) // BLOCK
    block_ends = jnp.cumsum(counts)
    block_starts = block_ends - counts
    row_index = jnp.arange(blocks_total * BLOCK, dtype=jnp.int32)
    member = jnp.sum(
        (block_ends[None, :] <= (row_index // BLOCK)[:, None]).astype(jnp.int32), axis=1
    )
    choose = (member[:, None] == jnp.arange(seq_count, dtype=jnp.int32)[None, :]).astype(jnp.int32)
    offset = row_index - BLOCK * jnp.sum(choose * block_starts[None, :], axis=1)
    length_row = jnp.sum(choose * lengths[None, :], axis=1)
    usable = (member < seq_count) & (offset < length_row)
    labels = jnp.where(usable, member, seq_count + row_index)
    position = jnp.where(usable, offset, 0)
    return (labels, position, usable)


def rope_tables(position):
    frequency = jnp.exp(
        jnp.arange(HEAD // 2, dtype=jnp.float32) * (-2.0 * math.log(10000.0) / HEAD)
    )
    angle_grid = position.astype(jnp.float32)[:, None] * frequency[None, :]
    return (jnp.cos(angle_grid)[:, None, :], jnp.sin(angle_grid)[:, None, :])


def rotate(vectors, cosine_table, sine_table):
    middle = HEAD // 2
    lower_half = vectors[..., :middle]
    upper_half = vectors[..., middle:]
    return jnp.concatenate(
        [
            lower_half * cosine_table - upper_half * sine_table,
            upper_half * cosine_table + lower_half * sine_table,
        ],
        axis=-1,
    )


def unrotate(grads, cosine_table, sine_table):
    middle = HEAD // 2
    lower_half = grads[..., :middle]
    upper_half = grads[..., middle:]
    return jnp.concatenate(
        [
            lower_half * cosine_table + upper_half * sine_table,
            upper_half * cosine_table - lower_half * sine_table,
        ],
        axis=-1,
    )


def rms_back(source, scale, gain, upstream):
    weighted = gain * upstream
    grad_in = scale * weighted - source * scale**3 * jnp.mean(
        weighted * source, axis=-1, keepdims=True
    )
    return (grad_in, jnp.sum(upstream * source * scale, axis=0))


def scores_for(query_group, key_group, allowed):
    raw_scores = (
        jnp.einsum("nqrd,nkd->nrqk", query_group, key_group, preferred_element_type=jnp.float32)
        * 0.125
    )
    return jnp.where(allowed[:, None], raw_scores, -1e30)


def adamw(master, grad, first, second, rate, decay):
    first_new = 0.9 * first + 0.1 * grad
    second_new = 0.95 * second + 0.05 * grad * grad
    update = first_new / (1.0 - 0.9**STEP) / (jnp.sqrt(second_new / (1.0 - 0.95**STEP)) + 1e-08)
    return (grad, first_new, second_new, master - rate * (update + decay * master))

MESH = pl.DeviceIdType.MESH
LOW = jnp.bfloat16


def exchange_kernel(count, axis, whole, *refs):
    number = len(whole)
    sources, targets = refs[:number], refs[number : 2 * number]
    send_sems, recv_sems, local_sems = refs[2 * number :]
    me = lax.axis_index(axis)
    barrier = pltpu.get_barrier_semaphore()
    for step in range(1, count):
        pl.semaphore_signal(
            barrier,
            inc=1,
            device_id={axis: lax.rem(me + step, count)},
            device_id_type=MESH,
        )
    pl.semaphore_wait(barrier, count - 1)
    copies = []
    for step in range(1, count):
        peer = lax.rem(me + step, count)
        for index in range(number):
            copy = pltpu.make_async_remote_copy(
                src_ref=sources[index] if whole[index] else sources[index].at[peer],
                dst_ref=targets[index].at[me],
                send_sem=send_sems.at[index, step - 1],
                recv_sem=recv_sems.at[index, step - 1],
                device_id={axis: peer},
                device_id_type=MESH,
            )
            copy.start()
            copies.append(copy)
    locals_ = []
    for index in range(number):
        copy = pltpu.make_async_copy(
            sources[index] if whole[index] else sources[index].at[me],
            targets[index].at[me],
            local_sems.at[index],
        )
        copy.start()
        locals_.append(copy)
    for copy in locals_:
        copy.wait()
    for copy in copies:
        copy.wait()


def exchange(ident, axis, whole, *arrays):
    count = lax.axis_size(axis)
    if any(array.shape[-2] % 16 for array in arrays):
        return [
            lax.all_gather(array, axis) if all_of_it else lax.all_to_all(array, axis, 0, 0)
            for array, all_of_it in zip(arrays, whole)
        ]
    shapes = [
        jax.ShapeDtypeStruct((count,) + array.shape[-2:], array.dtype) for array in arrays
    ]
    number = len(arrays)
    return pl.pallas_call(
        functools.partial(exchange_kernel, count, axis, tuple(whole)),
        out_shape=shapes,
        in_specs=[pl.BlockSpec(memory_space=pl.ANY)] * number,
        out_specs=[pl.BlockSpec(memory_space=pl.ANY)] * number,
        scratch_shapes=[
            pltpu.SemaphoreType.DMA((number, count - 1)),
            pltpu.SemaphoreType.DMA((number, count - 1)),
            pltpu.SemaphoreType.DMA((number,)),
        ],
        compiler_params=pltpu.CompilerParams(collective_id=ident, has_side_effects=True),
    )(*arrays)


def shared(ident, *arrays):
    return exchange(ident, "shard", [True] * len(arrays), *arrays)


def dealt(ident, *arrays):
    return exchange(ident, "shard", [False] * len(arrays), *arrays)


def to_pieces(array, count):
    rows, columns = array.shape
    return array.reshape(rows, count, columns // count).transpose(1, 0, 2)


def from_pieces(array):
    count, rows, columns = array.shape
    return array.transpose(1, 0, 2).reshape(rows, count * columns)


def added(array):
    return jnp.sum(array.astype(jnp.float32), axis=0)


def nt(left, right):
    return lax.dot_general(
        left, right, (((1,), (1,)), ((), ())), preferred_element_type=jnp.float32
    )


def nn(left, right):
    return jnp.dot(left, right, preferred_element_type=jnp.float32)


def tn(left, right):
    return lax.dot_general(
        left, right, (((0,), (0,)), ((), ())), preferred_element_type=jnp.float32
    )


def data_sum(array):
    return lax.psum_scatter(
        array.astype(LOW), "dp", scatter_dimension=0, tiled=True
    ).astype(jnp.float32)


def body(
    tokens,
    cotangent,
    seq_lengths,
    block_slot,
    qkv_master,
    qkv_first,
    qkv_second,
    out_master,
    out_first,
    out_second,
    gate_up_master,
    gate_up_first,
    gate_up_second,
    down_master,
    down_first,
    down_second,
    gains_master,
    gains_first,
    gains_second,
):
    lengths = seq_lengths[0]
    placing = block_slot[0]
    blocks_total = placing.shape[0]
    window = min(KBLK, blocks_total // 2)
    rows_local = tokens.shape[1]
    local_blocks = rows_local // BLOCK
    grouped = HEADS // KV_HEADS
    width_q = HEADS * HEAD
    width_kv = KV_HEADS * HEAD
    owner_count = lax.axis_size("shard")
    chunk = gate_up_master.shape[1] // owner_count
    span = down_master.shape[0] // (owner_count * chunk)
    qkv_t = lax.all_gather(qkv_master.T.astype(LOW), "dp", axis=0, tiled=True)
    out_t = lax.all_gather(out_master.T.astype(LOW), "dp", axis=0, tiled=True)
    gate_up_dealt, down_dealt = dealt(
        0,
        gate_up_master.T.astype(LOW).reshape(owner_count, chunk, -1),
        down_master.astype(LOW)
        .reshape(span, owner_count, chunk, -1)
        .transpose(1, 0, 2, 3)
        .reshape(owner_count, span * chunk, -1),
    )
    gate_up_t = lax.all_gather(from_pieces(gate_up_dealt), "dp", axis=0, tiled=True)
    down_t = lax.all_gather(
        down_dealt.reshape(owner_count * span * chunk, -1).T, "dp", axis=0, tiled=True
    )
    every = owner_count * rows_local
    labels_all, position_all, usable_all = layout(lengths, blocks_total)
    slot_index = jnp.arange(blocks_total, dtype=jnp.int32)
    local_slots = lax.axis_index("dp") * local_blocks + jnp.arange(local_blocks, dtype=jnp.int32)
    own_logical = jnp.sum(
        jnp.where(placing[None, :] == local_slots[:, None], slot_index[None, :], 0), axis=1
    )
    labels_table = labels_all.reshape(blocks_total, BLOCK)
    query_labels = jnp.take(labels_table, own_logical, axis=0)
    query_position = jnp.take(
        position_all.reshape(blocks_total, BLOCK), own_logical, axis=0
    ).reshape(rows_local)
    usable = (
        jnp.take(usable_all.reshape(blocks_total, BLOCK), own_logical, axis=0)
        .reshape(rows_local, 1)
        .astype(jnp.float32)
    )
    within = jnp.arange(BLOCK, dtype=jnp.int32)
    key_logical = own_logical[:, None] - (window - 1) + jnp.arange(window, dtype=jnp.int32)[None, :]
    key_present = key_logical >= 0
    key_clipped = jnp.maximum(key_logical, 0)
    key_slots = jnp.take(placing, key_clipped)
    key_labels = jnp.where(
        key_present[:, :, None], jnp.take(labels_table, key_clipped, axis=0), -1
    ).reshape(local_blocks, window * BLOCK)
    key_order = (key_logical[:, :, None] * BLOCK + within[None, None, :]).reshape(
        local_blocks, window * BLOCK
    )
    query_order = own_logical[:, None] * BLOCK + within[None, :]
    allowed = (query_labels[:, :, None] == key_labels[:, None, :]) & (
        key_order[:, None, :] <= query_order[:, :, None]
    )
    back_out = (cotangent[0].astype(jnp.float32) * usable).astype(LOW)
    source = tokens[0].astype(jnp.float32)
    scale_first = lax.rsqrt(jnp.mean(source * source, axis=-1, keepdims=True) + NORM_EPS)
    normed_first = (source * scale_first * gains_master[0]).astype(LOW)
    (normed_dealt,) = dealt(1, to_pieces(normed_first, owner_count))
    normed_slab = normed_dealt.reshape(every, -1)
    (projected_parts,) = dealt(
        2, nt(normed_slab, qkv_t).astype(LOW).reshape(owner_count, rows_local, -1)
    )
    projected = added(projected_parts)
    cosine_table, sine_table = rope_tables(query_position)
    queries = rotate(
        projected[:, :width_q].reshape(rows_local, HEADS, HEAD), cosine_table, sine_table
    ).astype(jnp.bfloat16)
    keys_rotated = rotate(
        projected[:, width_q : width_q + width_kv].reshape(rows_local, KV_HEADS, HEAD),
        cosine_table,
        sine_table,
    ).astype(jnp.bfloat16)
    values_local = projected[:, width_q + width_kv :].astype(jnp.bfloat16)
    keys_values = jnp.concatenate(
        [keys_rotated.reshape(rows_local, width_kv), values_local], axis=1
    )
    gathered = lax.all_gather(keys_values, "dp", axis=0, tiled=True)
    window_rows = jnp.take(
        gathered.reshape(blocks_total, BLOCK, 2 * width_kv), key_slots, axis=0
    ).reshape(local_blocks, window * BLOCK, 2 * width_kv)
    query_blocks = queries.reshape(local_blocks, BLOCK, KV_HEADS, grouped, HEAD)
    mixed_parts = []
    lse_parts = []
    for group_index in range(KV_HEADS):
        query_group = query_blocks[:, :, group_index]
        key_group = window_rows[:, :, group_index * HEAD : (group_index + 1) * HEAD]
        value_group = window_rows[
            :, :, width_kv + group_index * HEAD : width_kv + (group_index + 1) * HEAD
        ]
        scores = scores_for(query_group, key_group, allowed)
        top_score = jnp.max(scores, axis=-1, keepdims=True)
        shifted = jnp.exp(scores - top_score)
        totals = jnp.sum(shifted, axis=-1, keepdims=True)
        weights_low = (shifted / totals).astype(jnp.bfloat16)
        mixed_parts.append(
            jnp.einsum(
                "nrqk,nkd->nqrd", weights_low, value_group, preferred_element_type=jnp.float32
            )
        )
        lse_parts.append(top_score + jnp.log(totals))
    attended = jnp.stack(mixed_parts, axis=2).reshape(rows_local, width_q).astype(jnp.bfloat16)
    (attended_dealt,) = dealt(3, to_pieces(attended, owner_count))
    attended_slab = attended_dealt.reshape(every, -1)
    (mixed_sums,) = dealt(
        4, nt(attended_slab, out_t).astype(LOW).reshape(owner_count, rows_local, -1)
    )
    hidden_state = source + added(mixed_sums)
    scale_second = lax.rsqrt(
        jnp.mean(hidden_state * hidden_state, axis=-1, keepdims=True) + NORM_EPS
    )
    normed_second = (hidden_state * scale_second * gains_master[1]).astype(LOW)
    normed_all, back_out_all = shared(5, normed_second, back_out)
    normed_all = normed_all.reshape(every, -1)
    back_out_all = back_out_all.reshape(every, -1)
    gate_up = nt(normed_all, gate_up_t)
    units = gate_up.shape[1] // 2
    gate_part = gate_up[:, :units]
    up_part = gate_up[:, units:]
    sigmoid_gate = jax.nn.sigmoid(gate_part)
    silu_gate = gate_part * sigmoid_gate
    activated = (silu_gate * up_part).astype(LOW)
    back_act = nn(back_out_all, down_t)
    back_gate = back_act * up_part * sigmoid_gate * (1.0 + gate_part * (1.0 - sigmoid_gate))
    back_up = back_act * silu_gate
    back_gu = jnp.concatenate([back_gate, back_up], axis=1).astype(LOW)
    down_parts, second_parts = dealt(
        6,
        nt(activated, down_t).astype(LOW).reshape(owner_count, rows_local, -1),
        nn(back_gu, gate_up_t).astype(LOW).reshape(owner_count, rows_local, -1),
    )
    down_sum = data_sum(tn(back_out_all, activated))
    gate_up_sum = data_sum(tn(back_gu, normed_all))
    layer_out = ((hidden_state + added(down_parts)) * usable).astype(LOW)
    back_second = added(second_parts)
    norm_back, gain_second_grad = rms_back(hidden_state, scale_second, gains_master[1], back_second)
    back_hidden = back_out.astype(jnp.float32) + norm_back
    (back_hidden_all,) = shared(7, back_hidden.astype(LOW))
    back_hidden_all = back_hidden_all.reshape(every, -1)
    (back_att_pieces,) = dealt(
        8, nn(back_hidden_all, out_t).astype(LOW).reshape(owner_count, rows_local, -1)
    )
    out_sum = data_sum(tn(back_hidden_all, attended_slab))
    back_attended = from_pieces(back_att_pieces)
    back_blocks = back_attended.reshape(local_blocks, BLOCK, KV_HEADS, grouped, HEAD)
    query_grads = []
    key_grads = []
    value_grads = []
    for group_index in range(KV_HEADS):
        query_group = query_blocks[:, :, group_index]
        key_group = window_rows[:, :, group_index * HEAD : (group_index + 1) * HEAD]
        value_group = window_rows[
            :, :, width_kv + group_index * HEAD : width_kv + (group_index + 1) * HEAD
        ]
        scores = scores_for(query_group, key_group, allowed)
        weights_full = jnp.exp(scores - lse_parts[group_index])
        weights_low = weights_full.astype(jnp.bfloat16)
        upstream = back_blocks[:, :, group_index]
        back_weights = jnp.einsum(
            "nqrd,nkd->nrqk", upstream, value_group, preferred_element_type=jnp.float32
        )
        delta = jnp.sum(weights_full * back_weights, axis=-1, keepdims=True)
        back_scores = (weights_full * (back_weights - delta)).astype(jnp.bfloat16)
        query_grads.append(
            jnp.einsum("nrqk,nkd->nqrd", back_scores, key_group, preferred_element_type=jnp.float32)
            * 0.125
        )
        key_grads.append(
            jnp.einsum(
                "nrqk,nqrd->nkd", back_scores, query_group, preferred_element_type=jnp.float32
            )
            * 0.125
        )
        value_grads.append(
            jnp.einsum("nrqk,nqrd->nkd", weights_low, upstream, preferred_element_type=jnp.float32)
        )
    back_window = jnp.concatenate(key_grads + value_grads, axis=-1)
    back_slots = (
        jnp.zeros((blocks_total, BLOCK, 2 * width_kv), jnp.float32)
        .at[key_slots.reshape(-1)]
        .add(back_window.reshape(local_blocks * window, BLOCK, 2 * width_kv))
    )
    back_own = data_sum(back_slots.reshape(blocks_total * BLOCK, 2 * width_kv))
    query_back = unrotate(
        jnp.stack(query_grads, axis=2).reshape(rows_local, HEADS, HEAD), cosine_table, sine_table
    )
    key_back = unrotate(
        back_own[:, :width_kv].reshape(rows_local, KV_HEADS, HEAD), cosine_table, sine_table
    )
    back_proj = jnp.concatenate(
        [
            query_back.reshape(rows_local, width_q),
            key_back.reshape(rows_local, width_kv),
            back_own[:, width_kv:],
        ],
        axis=1,
    ).astype(jnp.bfloat16)
    (back_proj_all,) = shared(9, back_proj)
    back_proj_all = back_proj_all.reshape(every, -1)
    gate_up_back, down_back, first_pieces = dealt(
        10,
        to_pieces(gate_up_sum.astype(LOW), owner_count),
        down_sum.T.astype(LOW).reshape(owner_count, span * chunk, -1),
        nn(back_proj_all, qkv_t).astype(LOW).reshape(owner_count, rows_local, -1),
    )
    qkv_grad = data_sum(tn(back_proj_all, normed_slab)).T
    out_grad = out_sum.T
    gate_up_grad = gate_up_back.reshape(owner_count * chunk, -1).T.astype(jnp.float32)
    down_grad = (
        down_back.reshape(owner_count, span, chunk, -1)
        .transpose(1, 0, 2, 3)
        .reshape(down_master.shape)
        .astype(jnp.float32)
    )
    back_first = from_pieces(first_pieces).astype(jnp.float32)
    input_back, gain_first_grad = rms_back(source, scale_first, gains_master[0], back_first)
    input_grad = (back_hidden + input_back).astype(LOW)
    gains_grad = lax.psum(jnp.stack([gain_first_grad, gain_second_grad]), ("dp", "shard"))
    qkv_all = adamw(qkv_master, qkv_grad, qkv_first, qkv_second, MATRIX_RATE, WEIGHT_DECAY)
    out_all = adamw(out_master, out_grad, out_first, out_second, MATRIX_RATE, WEIGHT_DECAY)
    gate_up_all = adamw(
        gate_up_master, gate_up_grad, gate_up_first, gate_up_second, MATRIX_RATE, WEIGHT_DECAY
    )
    down_all = adamw(down_master, down_grad, down_first, down_second, MATRIX_RATE, WEIGHT_DECAY)
    gains_all = adamw(gains_master, gains_grad, gains_first, gains_second, GAIN_RATE, 0.0)
    return (
        layer_out[None],
        input_grad[None],
        qkv_all[0],
        qkv_all[1],
        qkv_all[2],
        qkv_all[3],
        out_all[0],
        out_all[1],
        out_all[2],
        out_all[3],
        gate_up_all[0],
        gate_up_all[1],
        gate_up_all[2],
        gate_up_all[3],
        down_all[0],
        down_all[1],
        down_all[2],
        down_all[3],
        gains_all[0],
        gains_all[1],
        gains_all[2],
        gains_all[3],
    )


def solution(mesh):
    in_specs = (
        P("shard", "dp", None),
        P("shard", "dp", None),
        P("shard", None),
        P("shard", None),
        P("shard", "dp"),
        P("shard", "dp"),
        P("shard", "dp"),
        P("shard", "dp"),
        P("shard", "dp"),
        P("shard", "dp"),
        P("shard", "dp"),
        P("shard", "dp"),
        P("shard", "dp"),
        P("shard", "dp"),
        P("shard", "dp"),
        P("shard", "dp"),
        P(),
        P(),
        P(),
    )
    out_specs = (
        P("shard", "dp", None),
        P("shard", "dp", None),
        P("shard", "dp"),
        P("shard", "dp"),
        P("shard", "dp"),
        P("shard", "dp"),
        P("shard", "dp"),
        P("shard", "dp"),
        P("shard", "dp"),
        P("shard", "dp"),
        P("shard", "dp"),
        P("shard", "dp"),
        P("shard", "dp"),
        P("shard", "dp"),
        P("shard", "dp"),
        P("shard", "dp"),
        P("shard", "dp"),
        P("shard", "dp"),
        P(),
        P(),
        P(),
        P(),
    )
    return jax.shard_map(body, mesh=mesh, in_specs=in_specs, out_specs=out_specs, check_vma=False)
```
